32 devices in a mesh: parts: 2 (over y), gx: 4 (over z), gy: 2 (over x), gz: 2 (over core).
Axes of the slice: x: 2, y: 2, z: 4, core: 2. Of those that a mesh axis runs over, the one named last changes fastest.
Arguments:
- e_adjoint: float32 [3, 64, 32, 256], P(None, ('parts', 'gx'), 'gz', 'gy'), parts along dimension 1, may hold values from -6 to 6
- h_adjoint: float32 [3, 64, 32, 256], P(None, ('parts', 'gx'), 'gz', 'gy'), parts along dimension 1, may hold values from -6 to 6
- forward_dft: bfloat16 [2, 16, 3, 64, 32, 256], P(None, None, None, ('parts', 'gx'), 'gz', 'gy'), parts along dimension 3, may hold values from -0.3984375 to 0.3984375
- material: int32 [64, 32, 256], P(('parts', 'gx'), 'gz', 'gy'), parts along dimension 0, may hold values from 0 to 3
- inv_permittivity: float32 [4], replicated, may hold values from 0.3 to 1
- conductivity: float32 [4], replicated, may hold values from 0.05 to 2
- omega: float32 [16], replicated, may hold values from 0.1 to 1.2
- freq_weight: float32 [16], replicated, may hold values from 0.3 to 1.5
- stencil: int32 [8, 64, 32, 256], P(None, ('parts', 'gx'), 'gz', 'gy'), parts along dimension 1, may hold values from 0 to 1023
- stencil_weight: bfloat16 [8, 64, 32, 256], P(None, ('parts', 'gx'), 'gz', 'gy'), parts along dimension 1, may hold values from 0.019897461 to 0.19921875
- owner_map: int32 [8, 2], P('parts'), parts along dimension 0, may hold values from 0 to 7
Outputs:
- e_final: float32 [3, 64, 32, 256], P(None, ('parts', 'gx'), 'gz', 'gy'), parts along dimension 1
- h_final: float32 [3, 64, 32, 256], P(None, ('parts', 'gx'), 'gz', 'gy'), parts along dimension 1
- material_grad: float32 [16, 1024], P(('parts', 'gx', 'gy'), 'gz'), parts along dimension 0
The draws below stay inside these ranges and needn't reach their ends.
There are 2 independent parts, one for each index of `parts`. The reference program is written for one: setup_inputs(seed, part) draws one part's arguments, and reference() takes and returns one part's arrays. A program takes and returns all parts, laid end to end along the dimension named above; an argument that names none is the same for every part. Nothing has to cross between parts.
All inputs are finite; a program needn't handle non-finite values.
Results may differ from the reference program's by a relative error of at most 0.0021.
Values sent between devices are 32-bit elements; how exact they have to be, the bound alone decides.
A program may use at most 64 MiB of HBM per device.

```python
import math
import jax
import jax.numpy as jnp
import numpy as np
from jax import lax

CX = 8
CY = 128
NZ = 32
NF = 16
NM = 4
K = 8
PS = 1024
STEPS = 4
NX = 32
NY = 256
OWNERS = 8
N_GX = 4
N_GY = 2


def place_ends(drawn, own_key, smallest, top_value):
    extent = drawn.shape
    index_at = [jax.random.randint(jax.random.fold_in(own_key, axis), (), 0, extent[axis]) for axis in range(len(extent))]
    drawn = drawn.at[tuple(index_at)].set(smallest)
    longest = extent.index(max(extent))
    index_at[longest] = (index_at[longest] + 1) % extent[longest]
    return drawn.at[tuple(index_at)].set(top_value)


def block_scale(stream_key, extent, pieces, least, high):
    def one(axis_at, blocks):
        heights = jax.random.uniform(jax.random.fold_in(jax.random.fold_in(stream_key, 6), axis_at), (blocks,), jnp.float32, least / len(pieces), high / len(pieces))
        return jnp.repeat(jnp.exp(heights), extent[axis_at] // blocks).reshape((-1,) + (1,) * (len(extent) - axis_at - 1))

    factor_of = one(*pieces[0])
    for cut in pieces[1:]:
        factor_of = factor_of * one(*cut)
    return factor_of


def cumulative_ranks(count, lean):
    portions = [(1 << 20) // math.isqrt(standing ** lean) + 1 for standing in range(1, count + 1)]
    width = 1 + sum(portions) // (1 << 30)
    return np.cumsum(np.array([max(1, weight // width) for weight in portions]))


def ranked_ids(own_key, shape, number_of, lean):
    listing = cumulative_ranks(number_of, lean)
    lot = jax.random.randint(jax.random.fold_in(own_key, 1), shape, 0, int(listing[number_of - 1]))
    standing = jnp.searchsorted(jnp.asarray(listing, jnp.int32), lot, side="right")
    return jax.random.permutation(jax.random.fold_in(own_key, 2), number_of)[standing].astype(jnp.int32)


def centred(stream_key, extent, width, reach, split=(), kind=jnp.bfloat16):
    entries = width * jax.random.normal(stream_key, extent, jnp.float32)
    if split:
        entries = entries * block_scale(stream_key, extent, split, -0.22, 0.18)
    return jnp.clip(entries, -reach, reach).astype(kind)


def setup_inputs(seed: int = 0, part: int = 0) -> dict:
    key_list = jax.random.split(jax.random.key(seed), 12)
    part_splits = jax.random.split(jax.random.fold_in(key_list[11], part), 12)
    e_adjoint = centred(part_splits[0], (3, NX, NZ, NY), 1.0, 6.0, ((1, 4), (2, 2), (3, 2)), jnp.float32)
    h_adjoint = centred(part_splits[1], (3, NX, NZ, NY), 1.0, 6.0, ((1, 4), (2, 2), (3, 2)), jnp.float32)
    forward_dft = centred(part_splits[2], (2, NF, 3, NX, NZ, NY), 0.05, 0.3984375, ((3, 4), (4, 2), (5, 2)))
    material = place_ends(jax.random.randint(part_splits[3], (NX, NZ, NY), 0, NM), jax.random.fold_in(part_splits[3], 1), 0, NM - 1).astype(jnp.int32)
    inv_permittivity = jnp.clip(jax.random.uniform(key_list[4], (NM,), jnp.float32, 0.3, 1.0), 0.3, 1.0)
    conductivity = jnp.clip(jnp.exp(jax.random.uniform(key_list[5], (NM,), jnp.float32, math.log(0.05), math.log(2.0))), 0.05, 2.0)
    omega = jnp.clip(jnp.exp(jax.random.uniform(key_list[6], (NF,), jnp.float32, math.log(0.1), math.log(1.2))), 0.1, 1.2)
    freq_weight = jnp.clip(jax.random.uniform(key_list[7], (NF,), jnp.float32, 0.3, 1.5), 0.3, 1.5)
    stencil = place_ends(jax.random.randint(part_splits[8], (K, NX, NZ, NY), 0, PS), jax.random.fold_in(part_splits[8], 1), 0, PS - 1).astype(jnp.int32)
    stencil_weight = jnp.clip(0.019897461 + 0.17932129 * jax.random.uniform(part_splits[9], (K, NX, NZ, NY), jnp.float32) ** block_scale(part_splits[9], (K, NX, NZ, NY), ((1, 4), (2, 2), (3, 2)), -0.2, 0.2), 0.019897461, 0.19921875).astype(jnp.bfloat16)
    owner_map = place_ends(ranked_ids(part_splits[10], (N_GX, N_GY), OWNERS, 2), jax.random.fold_in(part_splits[10], 3), 0, OWNERS - 1).astype(jnp.int32)
    return dict(e_adjoint=e_adjoint, h_adjoint=h_adjoint, forward_dft=forward_dft, material=material, inv_permittivity=inv_permittivity, conductivity=conductivity, omega=omega, freq_weight=freq_weight, stencil=stencil, stencil_weight=stencil_weight, owner_map=owner_map)


time_step = 0.55


def ahead_diff(field, axis):
    size = field.shape[axis]
    upper = jnp.zeros_like(lax.slice_in_dim(field, 0, 1, axis=axis))
    following = jnp.concatenate([lax.slice_in_dim(field, 1, size, axis=axis), upper], axis=axis)
    return following - field


def behind_diff(field, axis):
    size = field.shape[axis]
    lower = jnp.zeros_like(lax.slice_in_dim(field, 0, 1, axis=axis))
    previous = jnp.concatenate([lower, lax.slice_in_dim(field, 0, size - 1, axis=axis)], axis=axis)
    return field - previous


def curl_with(field, diff):
    comp_x, comp_y, comp_z = field[0], field[1], field[2]
    return jnp.stack([diff(comp_z, 2) - diff(comp_y, 1), diff(comp_x, 1) - diff(comp_z, 0), diff(comp_y, 0) - diff(comp_x, 2)])


def reference(e_adjoint, h_adjoint, forward_dft, material, inv_permittivity, conductivity, omega, freq_weight, stencil, stencil_weight, owner_map):
    inv_cell = jnp.take(inv_permittivity, material)
    cond_cell = jnp.take(conductivity, material)
    loss = cond_cell * (time_step * 0.5) * inv_cell
    decay = (1.0 - loss) / (1.0 + loss)
    drive = time_step * inv_cell / (1.0 + loss)
    times = (jnp.arange(STEPS) + 1).astype(jnp.float32) * time_step
    angles = times[:, None] * omega[None, :]
    phase = jnp.concatenate([freq_weight[None, :] * jnp.cos(angles), -freq_weight[None, :] * jnp.sin(angles)], axis=1).astype(jnp.bfloat16)
    weighted = jnp.dot(phase, forward_dft.reshape(2 * NF, -1), preferred_element_type=jnp.float32)
    weighted = weighted.reshape(STEPS, 3, NX, NZ, NY)
    e_now, h_now = e_adjoint, h_adjoint
    density = jnp.zeros((NX, NZ, NY), jnp.float32)
    for step in range(STEPS):
        h_now = h_now - time_step * curl_with(e_now, ahead_diff)
        e_now = decay * e_now + drive * curl_with(h_now, behind_diff)
        density = density + (e_now[0] * weighted[step, 0] + e_now[1] * weighted[step, 1] + e_now[2] * weighted[step, 2])
    brick_x = jnp.arange(NX, dtype=jnp.int32) // CX
    brick_y = jnp.arange(NY, dtype=jnp.int32) // CY
    brick = brick_x[:, None, None] * N_GY + brick_y[None, None, :]
    owner_cell = jnp.take(owner_map.reshape(-1), brick)
    target = owner_cell[None] * PS + stencil
    contrib = stencil_weight.astype(jnp.float32) * density[None]
    grad = jax.ops.segment_sum(contrib.reshape(-1), target.reshape(-1).astype(jnp.int32), num_segments=OWNERS * PS)
    return e_now, h_now, grad.reshape(OWNERS, PS)
```

```python
import functools

import jax
import jax.numpy as jnp
from jax import lax
from jax.experimental import pallas as pl
from jax.experimental.pallas import tpu as pltpu
from jax.sharding import PartitionSpec as P

PS = 1024
STEPS = 4
LOW = 32
time_step = 0.55
MESH = pl.DeviceIdType.MESH
F32 = jnp.float32
BF16 = jnp.bfloat16


def kernel(
    n_gx, n_gy, n_gz,
    phase, inv_eps, cond, owner_map,
    e_hbm, h_hbm, dft_hbm, mat_hbm, sten_hbm, w_hbm,
    e_ref, h_ref, grad_ref,
    dft, mat, sten, wgt, q_ref, decay_ref, drive_ref, g_ref,
    rows_ref, acc_ref, fold_ref,
    x_send, z_send, y_send, x_recv, z_recv, y_recv,
    p_send, p_recv,
    in_sems, send_sems, recv_sems, p_sems,
):
    freqs2, nc, nx, nz, ny = dft.shape
    points = sten.shape[0]
    part = lax.axis_index("parts")
    gx, gy, gz = lax.axis_index("gx"), lax.axis_index("gy"), lax.axis_index("gz")
    peers = n_gx * n_gy * n_gz
    me = (gx * n_gy + gy) * n_gz + gz

    def place(rank):
        return (part, rank // (n_gy * n_gz), (rank // n_gz) % n_gy, rank % n_gz)

    loads = [
        pltpu.make_async_copy(src, dst, in_sems.at[i])
        for i, (src, dst) in enumerate(
            [(e_hbm, e_ref), (h_hbm, h_ref), (mat_hbm, mat), (dft_hbm, dft), (sten_hbm, sten), (w_hbm, wgt)]
        )
    ]
    for load in loads:
        load.start()

    barrier = pltpu.get_barrier_semaphore()

    def greet(d, carry):
        pl.semaphore_signal(
            barrier, inc=1, device_id=place(lax.rem(me + d, peers)), device_id_type=MESH
        )
        return carry

    lax.fori_loop(1, peers, greet, 0)

    for has, slots, buf in (
        (gx < n_gx - 1, (0, 2, 4, 6), x_recv), (gx > 0, (1, 3, 5, 7), x_recv),
        (gz < n_gz - 1, (0, 2, 4, 6), z_recv), (gz > 0, (1, 3, 5, 7), z_recv),
        (gy < n_gy - 1, (0, 2, 4, 6), y_recv), (gy > 0, (1, 3, 5, 7), y_recv),
    ):
        @pl.when(jnp.logical_not(has))
        def _():
            for slot in slots:
                buf[slot] = jnp.zeros(buf.shape[1:], F32)

    pl.semaphore_wait(barrier, peers - 1)

    lane = lax.broadcasted_iota(jnp.int32, (nz, ny), 1)
    row = lax.broadcasted_iota(jnp.int32, (nz, ny), 0)

    def halo_copies(slot, ahead):
        by = -1 if ahead else 1

        def ends(at, size):
            low, high = at > 0, at < size - 1
            return (low, high) if ahead else (high, low)

        out = []
        for i, (snd, rcv, at, size, to) in enumerate((
            (x_send, x_recv, gx, n_gx, (part, gx + by, gy, gz)),
            (y_send, y_recv, gy, n_gy, (part, gx, gy + by, gz)),
            (z_send, z_recv, gz, n_gz, (part, gx, gy, gz + by)),
        )):
            copy = pltpu.make_async_remote_copy(
                src_ref=snd.at[slot], dst_ref=rcv.at[slot],
                send_sem=send_sems.at[slot, i], recv_sem=recv_sems.at[slot, i],
                device_id=to, device_id_type=MESH,
            )
            sends, receives = ends(at, size)
            out.append((copy, sends, receives))
        return out

    def start_halo(slot, ahead, ref):
        edge_x = 0 if ahead else nx - 1
        edge_z = 0 if ahead else nz - 1
        edge_y = 0 if ahead else ny - 1
        copies = halo_copies(slot, ahead)

        def go(which):
            copy, sends, _ = copies[which]

            @pl.when(sends)
            def _():
                copy.start()

        for c in range(2):
            x_send[slot, c] = ref[1 + c, edge_x]
        go(0)
        packed = jnp.zeros((nz, ny), F32)
        for c, comp in enumerate((0, 2)):
            for x in range(nx):
                at = c * nx + x
                moved = pltpu.roll(ref[comp, x], (at - edge_y) % ny, 1)
                packed = jnp.where(lane == at, moved, packed)
        y_send[slot] = packed
        go(1)
        for c in range(2):
            for x in range(nx):
                z_send[slot, pl.ds(c * nx + x, 1), :] = ref[c, x, pl.ds(edge_z, 1), :]
        go(2)

    def finish_halo(slot, ahead):
        for copy, _, receives in halo_copies(slot, ahead):
            @pl.when(receives)
            def _():
                copy.wait_recv()

    def curl(ref, slot, ahead, x, packed):
        def dx(comp):
            if ahead:
                nxt = ref[comp, x + 1] if x < nx - 1 else x_recv[slot, comp - 1]
                return nxt - ref[comp, x]
            prev = ref[comp, x - 1] if x > 0 else x_recv[slot, comp - 1]
            return ref[comp, x] - prev

        def dz(comp):
            halo = jnp.broadcast_to(z_recv[slot, pl.ds(comp * nx + x, 1), :], (nz, ny))
            here = ref[comp, x]
            if ahead:
                return jnp.where(row == nz - 1, halo, pltpu.roll(here, nz - 1, 0)) - here
            return here - jnp.where(row == 0, halo, pltpu.roll(here, 1, 0))

        def dy(comp):
            at = (comp // 2) * nx + x
            here = ref[comp, x]
            if ahead:
                halo = pltpu.roll(packed, (ny - 1 - at) % ny, 1)
                return jnp.where(lane == ny - 1, halo, pltpu.roll(here, ny - 1, 1)) - here
            halo = pltpu.roll(packed, (ny - at) % ny, 1)
            return here - jnp.where(lane == 0, halo, pltpu.roll(here, 1, 1))

        return dy(2) - dz(1), dz(0) - dx(2), dx(1) - dy(0)

    def weighted(c):
        def body(x, carry):
            sums = [jnp.zeros((nz, ny), F32) for _ in range(STEPS)]
            for f in range(freqs2):
                value = dft[f, c, x].astype(F32)
                for t in range(STEPS):
                    sums[t] = sums[t] + phase[t, f] * value
            for t in range(STEPS):
                q_ref[t, c, x] = sums[t]
            return carry

        lax.fori_loop(0, nx, body, 0)

    loads[0].wait()
    start_halo(0, True, e_ref)
    loads[1].wait()
    loads[2].wait()
    for x in range(nx):
        which = mat[x]
        inv_cell = jnp.zeros((nz, ny), F32)
        cond_cell = jnp.zeros((nz, ny), F32)
        for m in range(inv_eps.shape[0]):
            inv_cell = jnp.where(which == m, inv_eps[m], inv_cell)
            cond_cell = jnp.where(which == m, cond[m], cond_cell)
        loss = cond_cell * (time_step * 0.5) * inv_cell
        decay_ref[x] = (1.0 - loss) / (1.0 + loss)
        drive_ref[x] = time_step * inv_cell / (1.0 + loss)
        g_ref[x] = jnp.zeros((nz, ny), F32)
    loads[3].wait()
    weighted(0)
    for step in range(STEPS):
        finish_halo(2 * step, True)
        packed = y_recv[2 * step]
        for x in range(nx):
            parts = curl(e_ref, 2 * step, True, x, packed)
            for c in range(3):
                h_ref[c, x] = h_ref[c, x] - time_step * parts[c]
        start_halo(2 * step + 1, False, h_ref)
        if step == 0:
            weighted(1)
            weighted(2)
        finish_halo(2 * step + 1, False)
        packed = y_recv[2 * step + 1]
        for x in range(nx):
            parts = curl(h_ref, 2 * step + 1, False, x, packed)
            decay, drive = decay_ref[x], drive_ref[x]
            for c in range(3):
                e_ref[c, x] = decay * e_ref[c, x] + drive * parts[c]
        if step < STEPS - 1:
            start_halo(2 * step + 2, True, e_ref)
        for x in range(nx):
            g_ref[x] = g_ref[x] + (
                e_ref[0, x] * q_ref[step, 0, x]
                + e_ref[1, x] * q_ref[step, 1, x]
                + e_ref[2, x] * q_ref[step, 2, x]
            )

    loads[4].wait()
    loads[5].wait()
    high = PS // LOW
    ids = [
        (lax.broadcasted_iota(jnp.int32, (16, ny), 0) + 16 * i).astype(F32).astype(BF16)
        for i in range(2)
    ]
    zero = jnp.zeros((16, ny), BF16)
    one = jnp.ones((16, ny), BF16)
    groups = 4
    acc_ref[...] = jnp.zeros_like(acc_ref)

    def add_points(at, carry):
        k, x = at // nx, lax.rem(at, nx)
        index = sten[k, x]
        value = wgt[k, x].astype(F32) * g_ref[x]
        top = value.astype(BF16).astype(F32)
        rows_ref[0] = (index >> 5).astype(F32)
        rows_ref[1] = (index & (LOW - 1)).astype(F32)
        rows_ref[2] = top
        rows_ref[3] = value - top
        total = None
        for pair in range(nz // (2 * groups)):
            upper, rest, lower = [], [], []
            for half in range(2):
                ups, rests, lows = [], [], []
                for group in range(groups):
                    z = (group * (nz // (2 * groups)) + pair) * 2 + half
                    wide = [
                        jnp.broadcast_to(rows_ref[i, pl.ds(z, 1), :], (16, ny)).astype(BF16)
                        for i in range(4)
                    ]
                    for i in range(2):
                        hit = wide[0] == ids[i]
                        ups.append(jnp.where(hit, wide[2], zero))
                        rests.append(jnp.where(hit, wide[3], zero))
                        lows.append(jnp.where(wide[1] == ids[i], one, zero))
                upper.append(jnp.concatenate(ups, axis=0))
                rest.append(jnp.concatenate(rests, axis=0))
                lower.append(jnp.concatenate(lows, axis=0))
            left = jnp.concatenate(
                [jnp.concatenate(upper, axis=1), jnp.concatenate(rest, axis=1)], axis=0
            )
            right = jnp.concatenate(lower, axis=1)
            block = lax.dot_general(
                left, right, (((1,), (1,)), ((), ())), preferred_element_type=F32
            )
            total = block if total is None else total + block
        acc_ref[...] += total
        return carry

    lax.fori_loop(0, points * nx, add_points, 0)

    pieces = acc_ref[0 : groups * high, :] + acc_ref[groups * high :, :]
    width = groups * LOW
    lane_block = lax.broadcasted_iota(jnp.int32, (high, width), 1) // LOW
    row_block = lax.broadcasted_iota(jnp.int32, (high, width), 0) % groups
    summed = jnp.zeros((high, width), F32)
    for group in range(groups):
        summed = summed + jnp.where(
            lane_block == group, pieces[group * high : (group + 1) * high, :], 0.0
        )
    folded = summed
    for group in range(1, groups):
        folded = folded + pltpu.roll(summed, group * LOW, 1)
    folded = jnp.where(lane_block == row_block, folded, 0.0)
    fold_ref[...] = folded
    flat = fold_ref[pl.ds(0, high // groups, groups), :]
    for group in range(1, groups):
        flat = flat + fold_ref[pl.ds(group, high // groups, groups), :]
    tall = PS // n_gz // ny
    for i in range(n_gz):
        p_send[i] = flat[i * tall : (i + 1) * tall, :]

    def send_part(d, carry):
        to = lax.rem(me + d, peers)
        pltpu.make_async_remote_copy(
            src_ref=p_send.at[to % n_gz], dst_ref=p_recv.at[d - 1],
            send_sem=p_sems.at[0], recv_sem=p_sems.at[1],
            device_id=place(to), device_id_type=MESH,
        ).start()
        return carry

    lax.fori_loop(1, peers, send_part, 0)
    for slot in range(2 * STEPS):
        for copy, sends, _ in halo_copies(slot, slot % 2 == 0):
            @pl.when(sends)
            def _():
                copy.wait_send()
    pltpu.make_async_copy(p_recv, p_recv, p_sems.at[1]).wait()
    pltpu.make_async_copy(p_recv, p_recv, p_sems.at[0]).wait()

    my_owner = gx * n_gy + gy
    mine = jnp.where(owner_map[gx, gy] == my_owner, p_send[gz], 0.0)

    def add_part(d, total):
        brick = lax.rem(me - d + peers, peers) // n_gz
        owner = owner_map[brick // n_gy, brick % n_gy]
        return total + jnp.where(owner == my_owner, p_recv[d - 1], 0.0)

    mine = lax.fori_loop(1, peers, add_part, mine)
    for i in range(tall):
        grad_ref[:, i * ny : (i + 1) * ny] = mine[i : i + 1, :]


def on_device(
    e_adjoint, h_adjoint, forward_dft, material, inv_permittivity, conductivity,
    omega, freq_weight, stencil, stencil_weight, owner_map,
):
    nx, nz, ny = material.shape
    freqs = omega.shape[0]
    points = stencil.shape[0]
    n_gx, n_gy, n_gz = (lax.axis_size(a) for a in ("gx", "gy", "gz"))
    peers = n_gx * n_gy * n_gz
    times = (jnp.arange(STEPS) + 1).astype(F32) * time_step
    angles = times[:, None] * omega[None, :]
    phase = jnp.concatenate(
        [freq_weight[None, :] * jnp.cos(angles), -freq_weight[None, :] * jnp.sin(angles)], axis=1
    ).astype(BF16).astype(F32)
    dft = forward_dft.reshape(2 * freqs, 3, nx, nz, ny)
    smem = pl.BlockSpec(memory_space=pltpu.SMEM)
    hbm = pl.BlockSpec(memory_space=pl.ANY)
    vmem = pl.BlockSpec(memory_space=pltpu.VMEM)
    tall = PS // n_gz // ny
    slots = 2 * STEPS
    cell = (nx, nz, ny)
    return pl.pallas_call(
        functools.partial(kernel, n_gx, n_gy, n_gz),
        out_shape=(
            jax.ShapeDtypeStruct(e_adjoint.shape, F32),
            jax.ShapeDtypeStruct(h_adjoint.shape, F32),
            jax.ShapeDtypeStruct((1, PS // n_gz), F32),
        ),
        in_specs=[smem] * 4 + [hbm] * 6,
        out_specs=(vmem, vmem, vmem),
        scratch_shapes=[
            pltpu.VMEM(dft.shape, BF16),
            pltpu.VMEM(cell, jnp.int32),
            pltpu.VMEM(stencil.shape, jnp.int32),
            pltpu.VMEM(stencil_weight.shape, BF16),
            pltpu.VMEM((STEPS, 3) + cell, F32),
            pltpu.VMEM(cell, F32),
            pltpu.VMEM(cell, F32),
            pltpu.VMEM(cell, F32),
            pltpu.VMEM((4, nz, ny), F32),
            pltpu.VMEM((256, 128), F32),
            pltpu.VMEM((PS // LOW, 128), F32),
            pltpu.VMEM((slots, 2, nz, ny), F32),
            pltpu.VMEM((slots, 2 * nx, ny), F32),
            pltpu.VMEM((slots, nz, ny), F32),
            pltpu.VMEM((slots, 2, nz, ny), F32),
            pltpu.VMEM((slots, 2 * nx, ny), F32),
            pltpu.VMEM((slots, nz, ny), F32),
            pltpu.VMEM((n_gz, tall, ny), F32),
            pltpu.VMEM((peers - 1, tall, ny), F32),
            pltpu.SemaphoreType.DMA((6,)),
            pltpu.SemaphoreType.DMA((slots, 3)),
            pltpu.SemaphoreType.DMA((slots, 3)),
            pltpu.SemaphoreType.DMA((2,)),
        ],
        compiler_params=pltpu.CompilerParams(
            collective_id=0, has_side_effects=True, vmem_limit_bytes=32 * 1024 * 1024
        ),
    )(phase, inv_permittivity, conductivity, owner_map,
      e_adjoint, h_adjoint, dft, material, stencil, stencil_weight)


def solution(mesh):
    return jax.shard_map(
        on_device,
        mesh=mesh,
        in_specs=(
            P(None, ("parts", "gx"), "gz", "gy"),
            P(None, ("parts", "gx"), "gz", "gy"),
            P(None, None, None, ("parts", "gx"), "gz", "gy"),
            P(("parts", "gx"), "gz", "gy"),
            P(),
            P(),
            P(),
            P(),
            P(None, ("parts", "gx"), "gz", "gy"),
            P(None, ("parts", "gx"), "gz", "gy"),
            P("parts", None),
        ),
        out_specs=(
            P(None, ("parts", "gx"), "gz", "gy"),
            P(None, ("parts", "gx"), "gz", "gy"),
            P(("parts", "gx", "gy"), "gz"),
        ),
        check_vma=False,
    )
```

```python
import functools

import jax
import jax.numpy as jnp
from jax import lax
from jax.experimental import pallas as pl
from jax.experimental.pallas import tpu as pltpu
from jax.sharding import PartitionSpec as P

PS = 1024
STEPS = 4
LOW = 32
time_step = 0.55
MESH = pl.DeviceIdType.MESH
F32 = jnp.float32
BF16 = jnp.bfloat16


def kernel(
    n_gx, n_gy, n_gz,
    phase, inv_eps, cond, owner_map,
    e_hbm, h_hbm, dft_hbm, mat_hbm, sten_hbm, w_hbm,
    e_ref, h_ref, grad_ref,
    dft, mat, sten, wgt, q_ref, decay_ref, drive_ref, g_ref,
    rows_ref, acc_ref, fold_ref,
    x_send, z_send, y_send, x_recv, z_recv, y_recv,
    p_send, p_recv,
    in_sems, send_sems, recv_sems, p_sems,
):
    freqs2, nc, nx, nz, ny = dft.shape
    points = sten.shape[0]
    part = lax.axis_index("parts")
    gx, gy, gz = lax.axis_index("gx"), lax.axis_index("gy"), lax.axis_index("gz")
    peers = n_gx * n_gy * n_gz
    me = (gx * n_gy + gy) * n_gz + gz

    def place(rank):
        return (part, rank // (n_gy * n_gz), (rank // n_gz) % n_gy, rank % n_gz)

    loads = [
        pltpu.make_async_copy(src, dst, in_sems.at[i])
        for i, (src, dst) in enumerate(
            [(e_hbm, e_ref), (h_hbm, h_ref), (mat_hbm, mat), (dft_hbm, dft), (sten_hbm, sten), (w_hbm, wgt)]
        )
    ]
    for load in loads:
        load.start()

    barrier = pltpu.get_barrier_semaphore()

    def greet(d, carry):
        pl.semaphore_signal(
            barrier, inc=1, device_id=place(lax.rem(me + d, peers)), device_id_type=MESH
        )
        return carry

    lax.fori_loop(1, peers, greet, 0)

    for has, slots, buf in (
        (gx < n_gx - 1, (0, 2, 4, 6), x_recv), (gx > 0, (1, 3, 5, 7), x_recv),
        (gz < n_gz - 1, (0, 2, 4, 6), z_recv), (gz > 0, (1, 3, 5, 7), z_recv),
        (gy < n_gy - 1, (0, 2, 4, 6), y_recv), (gy > 0, (1, 3, 5, 7), y_recv),
    ):
        @pl.when(jnp.logical_not(has))
        def _():
            for slot in slots:
                buf[slot] = jnp.zeros(buf.shape[1:], F32)

    pl.semaphore_wait(barrier, peers - 1)

    lane = lax.broadcasted_iota(jnp.int32, (nz, ny), 1)
    row = lax.broadcasted_iota(jnp.int32, (nz, ny), 0)

    def halo_copies(slot, ahead):
        by = -1 if ahead else 1

        def ends(at, size):
            low, high = at > 0, at < size - 1
            return (low, high) if ahead else (high, low)

        out = []
        for i, (snd, rcv, at, size, to) in enumerate((
            (x_send, x_recv, gx, n_gx, (part, gx + by, gy, gz)),
            (y_send, y_recv, gy, n_gy, (part, gx, gy + by, gz)),
            (z_send, z_recv, gz, n_gz, (part, gx, gy, gz + by)),
        )):
            copy = pltpu.make_async_remote_copy(
                src_ref=snd.at[slot], dst_ref=rcv.at[slot],
                send_sem=send_sems.at[slot, i], recv_sem=recv_sems.at[slot, i],
                device_id=to, device_id_type=MESH,
            )
            sends, receives = ends(at, size)
            out.append((copy, sends, receives))
        return out

    def start_halo(slot, ahead, ref):
        edge_x = 0 if ahead else nx - 1
        edge_z = 0 if ahead else nz - 1
        edge_y = 0 if ahead else ny - 1
        copies = halo_copies(slot, ahead)

        def go(which):
            copy, sends, _ = copies[which]

            @pl.when(sends)
            def _():
                copy.start()

        for c in range(2):
            x_send[slot, c] = ref[1 + c, edge_x]
        go(0)
        packed = jnp.zeros((nz, ny), F32)
        for c, comp in enumerate((0, 2)):
            for x in range(nx):
                at = c * nx + x
                moved = pltpu.roll(ref[comp, x], (at - edge_y) % ny, 1)
                packed = jnp.where(lane == at, moved, packed)
        y_send[slot] = packed
        go(1)
        for c in range(2):
            for x in range(nx):
                z_send[slot, pl.ds(c * nx + x, 1), :] = ref[c, x, pl.ds(edge_z, 1), :]
        go(2)

    def finish_halo(slot, ahead):
        for copy, _, receives in halo_copies(slot, ahead):
            @pl.when(receives)
            def _():
                copy.wait_recv()

    def curl(ref, slot, ahead, x, packed):
        def dx(comp):
            if ahead:
                nxt = ref[comp, x + 1] if x < nx - 1 else x_recv[slot, comp - 1]
                return nxt - ref[comp, x]
            prev = ref[comp, x - 1] if x > 0 else x_recv[slot, comp - 1]
            return ref[comp, x] - prev

        def dz(comp):
            halo = jnp.broadcast_to(z_recv[slot, pl.ds(comp * nx + x, 1), :], (nz, ny))
            here = ref[comp, x]
            if ahead:
                return jnp.where(row == nz - 1, halo, pltpu.roll(here, nz - 1, 0)) - here
            return here - jnp.where(row == 0, halo, pltpu.roll(here, 1, 0))

        def dy(comp):
            at = (comp // 2) * nx + x
            here = ref[comp, x]
            if ahead:
                halo = pltpu.roll(packed, (ny - 1 - at) % ny, 1)
                return jnp.where(lane == ny - 1, halo, pltpu.roll(here, ny - 1, 1)) - here
            halo = pltpu.roll(packed, (ny - at) % ny, 1)
            return here - jnp.where(lane == 0, halo, pltpu.roll(here, 1, 1))

        return dy(2) - dz(1), dz(0) - dx(2), dx(1) - dy(0)

    def weighted(c):
        def body(x, carry):
            sums = [jnp.zeros((nz, ny), F32) for _ in range(STEPS)]
            for f in range(freqs2):
                value = dft[f, c, x].astype(F32)
                for t in range(STEPS):
                    sums[t] = sums[t] + phase[t, f] * value
            for t in range(STEPS):
                q_ref[t, c, x] = sums[t]
            return carry

        lax.fori_loop(0, nx, body, 0)

    loads[0].wait()
    start_halo(0, True, e_ref)
    loads[1].wait()
    loads[2].wait()
    for x in range(nx):
        which = mat[x]
        inv_cell = jnp.zeros((nz, ny), F32)
        cond_cell = jnp.zeros((nz, ny), F32)
        for m in range(inv_eps.shape[0]):
            inv_cell = jnp.where(which == m, inv_eps[m], inv_cell)
            cond_cell = jnp.where(which == m, cond[m], cond_cell)
        loss = cond_cell * (time_step * 0.5) * inv_cell
        decay_ref[x] = (1.0 - loss) / (1.0 + loss)
        drive_ref[x] = time_step * inv_cell / (1.0 + loss)
        g_ref[x] = jnp.zeros((nz, ny), F32)
    loads[3].wait()
    weighted(0)
    for step in range(STEPS):
        finish_halo(2 * step, True)
        packed = y_recv[2 * step]
        for x in range(nx):
            parts = curl(e_ref, 2 * step, True, x, packed)
            for c in range(3):
                h_ref[c, x] = h_ref[c, x] - time_step * parts[c]
        start_halo(2 * step + 1, False, h_ref)
        if step == 0:
            weighted(1)
            weighted(2)
        finish_halo(2 * step + 1, False)
        packed = y_recv[2 * step + 1]
        for x in range(nx):
            parts = curl(h_ref, 2 * step + 1, False, x, packed)
            decay, drive = decay_ref[x], drive_ref[x]
            for c in range(3):
                e_ref[c, x] = decay * e_ref[c, x] + drive * parts[c]
        if step < STEPS - 1:
            start_halo(2 * step + 2, True, e_ref)
        for x in range(nx):
            g_ref[x] = g_ref[x] + (
                e_ref[0, x] * q_ref[step, 0, x]
                + e_ref[1, x] * q_ref[step, 1, x]
                + e_ref[2, x] * q_ref[step, 2, x]
            )

    loads[4].wait()
    loads[5].wait()
    high = PS // LOW
    ids = [
        (lax.broadcasted_iota(jnp.int32, (16, ny), 0) + 16 * i).astype(F32).astype(BF16)
        for i in range(2)
    ]
    zero = jnp.zeros((16, ny), BF16)
    one = jnp.ones((16, ny), BF16)
    groups = 4
    acc_ref[...] = jnp.zeros_like(acc_ref)

    def add_points(x, carry):
        total = None
        for k in range(points):
            index = sten[k, x]
            value = wgt[k, x].astype(F32) * g_ref[x]
            top = value.astype(BF16).astype(F32)
            rows_ref[k, 0] = (index >> 5).astype(F32)
            rows_ref[k, 1] = (index & (LOW - 1)).astype(F32)
            rows_ref[k, 2] = top
            rows_ref[k, 3] = value - top
        for k in range(points):
            for pair in range(nz // (2 * groups)):
                upper, rest, lower = [], [], []
                for half in range(2):
                    ups, rests, lows = [], [], []
                    for group in range(groups):
                        z = (group * (nz // (2 * groups)) + pair) * 2 + half
                        wide = [
                            jnp.broadcast_to(rows_ref[k, i, pl.ds(z, 1), :], (16, ny)).astype(BF16)
                            for i in range(4)
                        ]
                        for i in range(2):
                            hit = wide[0] == ids[i]
                            ups.append(jnp.where(hit, wide[2], zero))
                            rests.append(jnp.where(hit, wide[3], zero))
                            lows.append(jnp.where(wide[1] == ids[i], one, zero))
                    upper.append(jnp.concatenate(ups, axis=0))
                    rest.append(jnp.concatenate(rests, axis=0))
                    lower.append(jnp.concatenate(lows, axis=0))
                left = jnp.concatenate(
                    [jnp.concatenate(upper, axis=1), jnp.concatenate(rest, axis=1)], axis=0
                )
                right = jnp.concatenate(lower, axis=1)
                block = lax.dot_general(
                    left, right, (((1,), (1,)), ((), ())), preferred_element_type=F32
                )
                total = block if total is None else total + block
        acc_ref[...] += total
        return carry

    lax.fori_loop(0, nx, add_points, 0)

    pieces = acc_ref[0 : groups * high, :] + acc_ref[groups * high :, :]
    width = groups * LOW
    lane_block = lax.broadcasted_iota(jnp.int32, (high, width), 1) // LOW
    row_block = lax.broadcasted_iota(jnp.int32, (high, width), 0) % groups
    summed = jnp.zeros((high, width), F32)
    for group in range(groups):
        summed = summed + jnp.where(
            lane_block == group, pieces[group * high : (group + 1) * high, :], 0.0
        )
    folded = summed
    for group in range(1, groups):
        folded = folded + pltpu.roll(summed, group * LOW, 1)
    folded = jnp.where(lane_block == row_block, folded, 0.0)
    fold_ref[...] = folded
    flat = fold_ref[pl.ds(0, high // groups, groups), :]
    for group in range(1, groups):
        flat = flat + fold_ref[pl.ds(group, high // groups, groups), :]
    tall = PS // n_gz // ny
    for i in range(n_gz):
        p_send[i] = flat[i * tall : (i + 1) * tall, :]

    def send_part(d, carry):
        to = lax.rem(me + d, peers)
        pltpu.make_async_remote_copy(
            src_ref=p_send.at[to % n_gz], dst_ref=p_recv.at[d - 1],
            send_sem=p_sems.at[0], recv_sem=p_sems.at[1],
            device_id=place(to), device_id_type=MESH,
        ).start()
        return carry

    lax.fori_loop(1, peers, send_part, 0)
    for slot in range(2 * STEPS):
        for copy, sends, _ in halo_copies(slot, slot % 2 == 0):
            @pl.when(sends)
            def _():
                copy.wait_send()
    pltpu.make_async_copy(p_recv, p_recv, p_sems.at[1]).wait()
    pltpu.make_async_copy(p_recv, p_recv, p_sems.at[0]).wait()

    my_owner = gx * n_gy + gy
    mine = jnp.where(owner_map[gx, gy] == my_owner, p_send[gz], 0.0)

    def add_part(d, total):
        brick = lax.rem(me - d + peers, peers) // n_gz
        owner = owner_map[brick // n_gy, brick % n_gy]
        return total + jnp.where(owner == my_owner, p_recv[d - 1], 0.0)

    mine = lax.fori_loop(1, peers, add_part, mine)
    for i in range(tall):
        grad_ref[:, i * ny : (i + 1) * ny] = mine[i : i + 1, :]


def on_device(
    e_adjoint, h_adjoint, forward_dft, material, inv_permittivity, conductivity,
    omega, freq_weight, stencil, stencil_weight, owner_map,
):
    nx, nz, ny = material.shape
    freqs = omega.shape[0]
    points = stencil.shape[0]
    n_gx, n_gy, n_gz = (lax.axis_size(a) for a in ("gx", "gy", "gz"))
    peers = n_gx * n_gy * n_gz
    times = (jnp.arange(STEPS) + 1).astype(F32) * time_step
    angles = times[:, None] * omega[None, :]
    phase = jnp.concatenate(
        [freq_weight[None, :] * jnp.cos(angles), -freq_weight[None, :] * jnp.sin(angles)], axis=1
    ).astype(BF16).astype(F32)
    dft = forward_dft.reshape(2 * freqs, 3, nx, nz, ny)
    smem = pl.BlockSpec(memory_space=pltpu.SMEM)
    hbm = pl.BlockSpec(memory_space=pl.ANY)
    vmem = pl.BlockSpec(memory_space=pltpu.VMEM)
    tall = PS // n_gz // ny
    slots = 2 * STEPS
    cell = (nx, nz, ny)
    return pl.pallas_call(
        functools.partial(kernel, n_gx, n_gy, n_gz),
        out_shape=(
            jax.ShapeDtypeStruct(e_adjoint.shape, F32),
            jax.ShapeDtypeStruct(h_adjoint.shape, F32),
            jax.ShapeDtypeStruct((1, PS // n_gz), F32),
        ),
        in_specs=[smem] * 4 + [hbm] * 6,
        out_specs=(vmem, vmem, vmem),
        scratch_shapes=[
            pltpu.VMEM(dft.shape, BF16),
            pltpu.VMEM(cell, jnp.int32),
            pltpu.VMEM(stencil.shape, jnp.int32),
            pltpu.VMEM(stencil_weight.shape, BF16),
            pltpu.VMEM((STEPS, 3) + cell, F32),
            pltpu.VMEM(cell, F32),
            pltpu.VMEM(cell, F32),
            pltpu.VMEM(cell, F32),
            pltpu.VMEM((points, 4, nz, ny), F32),
            pltpu.VMEM((256, 128), F32),
            pltpu.VMEM((PS // LOW, 128), F32),
            pltpu.VMEM((slots, 2, nz, ny), F32),
            pltpu.VMEM((slots, 2 * nx, ny), F32),
            pltpu.VMEM((slots, nz, ny), F32),
            pltpu.VMEM((slots, 2, nz, ny), F32),
            pltpu.VMEM((slots, 2 * nx, ny), F32),
            pltpu.VMEM((slots, nz, ny), F32),
            pltpu.VMEM((n_gz, tall, ny), F32),
            pltpu.VMEM((peers - 1, tall, ny), F32),
            pltpu.SemaphoreType.DMA((6,)),
            pltpu.SemaphoreType.DMA((slots, 3)),
            pltpu.SemaphoreType.DMA((slots, 3)),
            pltpu.SemaphoreType.DMA((2,)),
        ],
        compiler_params=pltpu.CompilerParams(
            collective_id=0, has_side_effects=True, vmem_limit_bytes=60 * 1024 * 1024
        ),
    )(phase, inv_permittivity, conductivity, owner_map,
      e_adjoint, h_adjoint, dft, material, stencil, stencil_weight)


def solution(mesh):
    return jax.shard_map(
        on_device,
        mesh=mesh,
        in_specs=(
            P(None, ("parts", "gx"), "gz", "gy"),
            P(None, ("parts", "gx"), "gz", "gy"),
            P(None, None, None, ("parts", "gx"), "gz", "gy"),
            P(("parts", "gx"), "gz", "gy"),
            P(),
            P(),
            P(),
            P(),
            P(None, ("parts", "gx"), "gz", "gy"),
            P(None, ("parts", "gx"), "gz", "gy"),
            P("parts", None),
        ),
        out_specs=(
            P(None, ("parts", "gx"), "gz", "gy"),
            P(None, ("parts", "gx"), "gz", "gy"),
            P(("parts", "gx", "gy"), "gz"),
        ),
        check_vma=False,
    )
```

```python
import functools

import jax
import jax.numpy as jnp
from jax import lax
from jax.experimental import pallas as pl
from jax.experimental.pallas import tpu as pltpu
from jax.sharding import PartitionSpec as P

PS = 1024
STEPS = 4
LOW = 32
time_step = 0.55
MESH = pl.DeviceIdType.MESH
F32 = jnp.float32
BF16 = jnp.bfloat16


def kernel(
    n_gx, n_gy, n_gz,
    phase, inv_eps, cond, owner_map,
    e_hbm, h_hbm, dft_hbm, mat_hbm, sten_hbm, w_hbm,
    e_ref, h_ref, grad_ref,
    dft, mat, sten, wgt, q_ref, decay_ref, drive_ref, g_ref,
    rows_ref, acc_ref, fold_ref,
    x_send, z_send, y_send, x_recv, z_recv, y_recv,
    row_send, col_send, row_recv, col_recv,
    p_send, p_recv,
    in_sems, send_sems, recv_sems, edge_sems, p_sems,
):
    freqs2, nc, nx, nz, ny = dft.shape
    points = sten.shape[0]
    part = lax.axis_index("parts")
    gx, gy, gz = lax.axis_index("gx"), lax.axis_index("gy"), lax.axis_index("gz")
    peers = n_gx * n_gy * n_gz
    me = (gx * n_gy + gy) * n_gz + gz

    def place(rank):
        return (part, rank // (n_gy * n_gz), (rank // n_gz) % n_gy, rank % n_gz)

    loads = [
        pltpu.make_async_copy(src, dst, in_sems.at[i])
        for i, (src, dst) in enumerate(
            [(e_hbm, e_ref), (h_hbm, h_ref), (mat_hbm, mat), (dft_hbm, dft), (sten_hbm, sten), (w_hbm, wgt)]
        )
    ]
    for load in loads:
        load.start()

    barrier = pltpu.get_barrier_semaphore()

    def greet(d, carry):
        pl.semaphore_signal(
            barrier, inc=1, device_id=place(lax.rem(me + d, peers)), device_id_type=MESH
        )
        return carry

    lax.fori_loop(1, peers, greet, 0)

    for has, slots, buf in (
        (gx < n_gx - 1, (0, 2, 4, 6), x_recv), (gx > 0, (1, 3, 5, 7), x_recv),
        (gz < n_gz - 1, (0, 2, 4, 6), z_recv), (gz > 0, (1, 3, 5, 7), z_recv),
        (gy < n_gy - 1, (0, 2, 4, 6), y_recv), (gy > 0, (1, 3, 5, 7), y_recv),
    ):
        @pl.when(jnp.logical_not(has))
        def _():
            for slot in slots:
                buf[slot] = jnp.zeros(buf.shape[1:], F32)

    low = (gx > 0, gy > 0, gz > 0)
    high_side = (gx < n_gx - 1, gy < n_gy - 1, gz < n_gz - 1)
    edges = (
        (row_send, row_recv, 0, 0, 2), (row_send, row_recv, 1, 1, 2),
        (col_send, col_recv, 0, 0, 1), (col_send, col_recv, 1, 1, 0),
    )
    for _, rcv, which, up, down in edges:
        @pl.when(jnp.logical_not(low[up] & high_side[down]))
        def _():
            for step in range(STEPS):
                rcv[step, which] = jnp.zeros(rcv.shape[2:], F32)

    pl.semaphore_wait(barrier, peers - 1)

    lane = lax.broadcasted_iota(jnp.int32, (nz, ny), 1)
    row = lax.broadcasted_iota(jnp.int32, (nz, ny), 0)

    def halo_copies(slot, ahead):
        by = -1 if ahead else 1

        def ends(at, size):
            low, high = at > 0, at < size - 1
            return (low, high) if ahead else (high, low)

        out = []
        for i, (snd, rcv, at, size, to) in enumerate((
            (x_send, x_recv, gx, n_gx, (part, gx + by, gy, gz)),
            (y_send, y_recv, gy, n_gy, (part, gx, gy + by, gz)),
            (z_send, z_recv, gz, n_gz, (part, gx, gy, gz + by)),
        )):
            copy = pltpu.make_async_remote_copy(
                src_ref=snd.at[slot], dst_ref=rcv.at[slot],
                send_sem=send_sems.at[slot, i], recv_sem=recv_sems.at[slot, i],
                device_id=to, device_id_type=MESH,
            )
            sends, receives = ends(at, size)
            out.append((copy, sends, receives))
        return out

    def edge_copies(step):
        out = []
        for i, (snd, rcv, which, up, down) in enumerate(edges):
            to = [gx, gy, gz]
            to[up] = to[up] + 1
            to[down] = to[down] - 1
            copy = pltpu.make_async_remote_copy(
                src_ref=snd.at[step, which], dst_ref=rcv.at[step, which],
                send_sem=edge_sems.at[0, step, i], recv_sem=edge_sems.at[1, step, i],
                device_id=(part, *to), device_id_type=MESH,
            )
            out.append((copy, high_side[up] & low[down], low[up] & high_side[down]))
        return out

    def go(entry):
        @pl.when(entry[1])
        def _():
            entry[0].start()

    def arrive(entry):
        @pl.when(entry[2])
        def _():
            entry[0].wait_recv()

    def start_z(slot, ahead, ref):
        edge_z = 0 if ahead else nz - 1
        for c in range(2):
            for x in range(nx):
                z_send[slot, pl.ds(c * nx + x, 1), :] = ref[c, x, pl.ds(edge_z, 1), :]
        go(halo_copies(slot, ahead)[2])

    def inner_z(comp, x):
        here = e_ref[comp, x]
        return jnp.where(row == nz - 1, 0.0, pltpu.roll(here, nz - 1, 0)) - here

    def start_step(step):
        down, up, lines = halo_copies(2 * step, True), halo_copies(2 * step + 1, False), edge_copies(step)
        end = nx - 1
        for c in range(2):
            x_send[2 * step, c] = e_ref[1 + c, 0]
        go(down[0])
        here = e_ref[0, end]
        turned = pltpu.roll(here, ny - 1, 1)
        x_send[2 * step + 1, 0] = h_ref[1, end] - time_step * (inner_z(0, end) + e_ref[2, end])
        x_send[2 * step + 1, 1] = h_ref[2, end] + time_step * (
            e_ref[1, end] + (jnp.where(lane == ny - 1, 0.0, turned) - here)
        )
        go(up[0])
        col_send[step, 0] = turned
        go(lines[2])
        col_send[step, 1] = pltpu.roll(e_ref[1, 0], (2 * nx - ny) % ny, 1)
        go(lines[3])
        row_send[step, 0] = jnp.broadcast_to(e_ref[0, end, pl.ds(0, 1), :], (8, ny))
        go(lines[0])
        packed = jnp.zeros((nz, ny), F32)
        for c, comp in enumerate((0, 2)):
            for x in range(nx):
                at = c * nx + x
                packed = jnp.where(lane == at, pltpu.roll(e_ref[comp, x], at, 1), packed)
        y_send[2 * step] = packed
        go(down[1])
        packed = jnp.zeros((nz, ny), F32)
        for c in range(2):
            for x in range(nx):
                at = c * nx + x
                if c == 0:
                    value = h_ref[0, x] + time_step * (e_ref[2, x] + inner_z(1, x))
                else:
                    change = e_ref[1, x + 1] - e_ref[1, x] if x < end else -e_ref[1, x]
                    value = h_ref[2, x] - time_step * (change + e_ref[0, x])
                packed = jnp.where(lane == at, pltpu.roll(value, at + 1, 1), packed)
        y_send[2 * step + 1] = packed
        go(up[1])
        line = jnp.zeros((8, ny), F32)
        for x in range(nx):
            line = jnp.where(
                lane[0:8] == x, pltpu.roll(e_ref[1, x, pl.ds(0, 8), :], x + 1, 1), line
            )
        row_send[step, 1] = line
        go(lines[1])
        start_z(2 * step, True, e_ref)

    def finish_step(step):
        for entry in halo_copies(2 * step, True):
            arrive(entry)
        for entry in halo_copies(2 * step + 1, False)[:2] + edge_copies(step):
            arrive(entry)
        slot = 2 * step + 1
        last_row, last_lane = row == nz - 1, lane == ny - 1
        line = jnp.broadcast_to(row_recv[step, 0, pl.ds(0, 1), :], (nz, ny))
        plane = x_recv[slot, 0] + time_step * (e_ref[2, 0] - jnp.where(last_row, line, 0.0))
        x_recv[slot, 0] = jnp.where(gx > 0, plane, 0.0)
        plane = x_recv[slot, 1] - time_step * (
            e_ref[1, 0] - jnp.where(last_lane, col_recv[step, 0], 0.0)
        )
        x_recv[slot, 1] = jnp.where(gx > 0, plane, 0.0)
        own = y_send[2 * step]
        own = jnp.where(lane < nx, -pltpu.roll(own, ny - nx, 1), pltpu.roll(own, nx, 1))
        line = jnp.broadcast_to(row_recv[step, 1, pl.ds(0, 1), :], (nz, ny))
        own = own + jnp.where(last_row & (lane < nx), line, 0.0)
        own = own - jnp.where(lane == 2 * nx - 1, col_recv[step, 1], 0.0)
        y_recv[slot] = jnp.where(gy > 0, y_recv[slot] + time_step * own, 0.0)

    def curl(ref, slot, ahead, x, packed):
        def dx(comp):
            if ahead:
                nxt = ref[comp, x + 1] if x < nx - 1 else x_recv[slot, comp - 1]
                return nxt - ref[comp, x]
            prev = ref[comp, x - 1] if x > 0 else x_recv[slot, comp - 1]
            return ref[comp, x] - prev

        def dz(comp):
            halo = jnp.broadcast_to(z_recv[slot, pl.ds(comp * nx + x, 1), :], (nz, ny))
            here = ref[comp, x]
            if ahead:
                return jnp.where(row == nz - 1, halo, pltpu.roll(here, nz - 1, 0)) - here
            return here - jnp.where(row == 0, halo, pltpu.roll(here, 1, 0))

        def dy(comp):
            at = (comp // 2) * nx + x
            here = ref[comp, x]
            if ahead:
                halo = pltpu.roll(packed, (ny - 1 - at) % ny, 1)
                return jnp.where(lane == ny - 1, halo, pltpu.roll(here, ny - 1, 1)) - here
            halo = pltpu.roll(packed, (ny - at) % ny, 1)
            return here - jnp.where(lane == 0, halo, pltpu.roll(here, 1, 1))

        return dy(2) - dz(1), dz(0) - dx(2), dx(1) - dy(0)

    def weighted(c):
        def body(x, carry):
            sums = [jnp.zeros((nz, ny), F32) for _ in range(STEPS)]
            for f in range(freqs2):
                value = dft[f, c, x].astype(F32)
                for t in range(STEPS):
                    sums[t] = sums[t] + phase[t, f] * value
            for t in range(STEPS):
                q_ref[t, c, x] = sums[t]
            return carry

        lax.fori_loop(0, nx, body, 0)

    loads[0].wait()
    loads[1].wait()
    start_step(0)
    loads[2].wait()
    for x in range(nx):
        which = mat[x]
        inv_cell = jnp.zeros((nz, ny), F32)
        cond_cell = jnp.zeros((nz, ny), F32)
        for m in range(inv_eps.shape[0]):
            inv_cell = jnp.where(which == m, inv_eps[m], inv_cell)
            cond_cell = jnp.where(which == m, cond[m], cond_cell)
        loss = cond_cell * (time_step * 0.5) * inv_cell
        decay_ref[x] = (1.0 - loss) / (1.0 + loss)
        drive_ref[x] = time_step * inv_cell / (1.0 + loss)
        g_ref[x] = jnp.zeros((nz, ny), F32)
    loads[3].wait()
    for c in range(3):
        weighted(c)
    for step in range(STEPS):
        finish_step(step)
        packed = y_recv[2 * step]
        for x in range(nx):
            parts = curl(e_ref, 2 * step, True, x, packed)
            for c in range(3):
                h_ref[c, x] = h_ref[c, x] - time_step * parts[c]
        start_z(2 * step + 1, False, h_ref)
        arrive(halo_copies(2 * step + 1, False)[2])
        packed = y_recv[2 * step + 1]
        for x in range(nx):
            parts = curl(h_ref, 2 * step + 1, False, x, packed)
            decay, drive = decay_ref[x], drive_ref[x]
            for c in range(3):
                e_ref[c, x] = decay * e_ref[c, x] + drive * parts[c]
        if step < STEPS - 1:
            start_step(step + 1)
        for x in range(nx):
            g_ref[x] = g_ref[x] + (
                e_ref[0, x] * q_ref[step, 0, x]
                + e_ref[1, x] * q_ref[step, 1, x]
                + e_ref[2, x] * q_ref[step, 2, x]
            )

    loads[4].wait()
    loads[5].wait()
    high = PS // LOW
    ids = [
        (lax.broadcasted_iota(jnp.int32, (16, ny), 0) + 16 * i).astype(F32).astype(BF16)
        for i in range(2)
    ]
    zero = jnp.zeros((16, ny), BF16)
    one = jnp.ones((16, ny), BF16)
    groups = 4
    acc_ref[...] = jnp.zeros_like(acc_ref)

    def add_points(x, carry):
        total = None
        for k in range(points):
            index = sten[k, x]
            value = wgt[k, x].astype(F32) * g_ref[x]
            top = value.astype(BF16).astype(F32)
            rows_ref[k, 0] = (index >> 5).astype(F32)
            rows_ref[k, 1] = (index & (LOW - 1)).astype(F32)
            rows_ref[k, 2] = top
            rows_ref[k, 3] = value - top
        for k in range(points):
            for pair in range(nz // (2 * groups)):
                upper, rest, lower = [], [], []
                for half in range(2):
                    ups, rests, lows = [], [], []
                    for group in range(groups):
                        z = (group * (nz // (2 * groups)) + pair) * 2 + half
                        wide = [
                            jnp.broadcast_to(rows_ref[k, i, pl.ds(z, 1), :], (16, ny)).astype(BF16)
                            for i in range(4)
                        ]
                        for i in range(2):
                            hit = wide[0] == ids[i]
                            ups.append(jnp.where(hit, wide[2], zero))
                            rests.append(jnp.where(hit, wide[3], zero))
                            lows.append(jnp.where(wide[1] == ids[i], one, zero))
                    upper.append(jnp.concatenate(ups, axis=0))
                    rest.append(jnp.concatenate(rests, axis=0))
                    lower.append(jnp.concatenate(lows, axis=0))
                left = jnp.concatenate(
                    [jnp.concatenate(upper, axis=1), jnp.concatenate(rest, axis=1)], axis=0
                )
                right = jnp.concatenate(lower, axis=1)
                block = lax.dot_general(
                    left, right, (((1,), (1,)), ((), ())), preferred_element_type=F32
                )
                total = block if total is None else total + block
        acc_ref[...] += total
        return carry

    lax.fori_loop(0, nx, add_points, 0)

    pieces = acc_ref[0 : groups * high, :] + acc_ref[groups * high :, :]
    width = groups * LOW
    lane_block = lax.broadcasted_iota(jnp.int32, (high, width), 1) // LOW
    row_block = lax.broadcasted_iota(jnp.int32, (high, width), 0) % groups
    summed = jnp.zeros((high, width), F32)
    for group in range(groups):
        summed = summed + jnp.where(
            lane_block == group, pieces[group * high : (group + 1) * high, :], 0.0
        )
    folded = summed
    for group in range(1, groups):
        folded = folded + pltpu.roll(summed, group * LOW, 1)
    folded = jnp.where(lane_block == row_block, folded, 0.0)
    fold_ref[...] = folded
    flat = fold_ref[pl.ds(0, high // groups, groups), :]
    for group in range(1, groups):
        flat = flat + fold_ref[pl.ds(group, high // groups, groups), :]
    tall = PS // n_gz // ny
    for i in range(n_gz):
        p_send[i] = flat[i * tall : (i + 1) * tall, :]

    def send_part(d, carry):
        to = lax.rem(me + d, peers)
        pltpu.make_async_remote_copy(
            src_ref=p_send.at[to % n_gz], dst_ref=p_recv.at[d - 1],
            send_sem=p_sems.at[0], recv_sem=p_sems.at[1],
            device_id=place(to), device_id_type=MESH,
        ).start()
        return carry

    lax.fori_loop(1, peers, send_part, 0)
    for slot in range(2 * STEPS):
        for copy, sends, _ in halo_copies(slot, slot % 2 == 0):
            @pl.when(sends)
            def _():
                copy.wait_send()
    for step in range(STEPS):
        for copy, sends, _ in edge_copies(step):
            @pl.when(sends)
            def _():
                copy.wait_send()
    pltpu.make_async_copy(p_recv, p_recv, p_sems.at[1]).wait()
    pltpu.make_async_copy(p_recv, p_recv, p_sems.at[0]).wait()

    my_owner = gx * n_gy + gy
    mine = jnp.where(owner_map[gx, gy] == my_owner, p_send[gz], 0.0)

    def add_part(d, total):
        brick = lax.rem(me - d + peers, peers) // n_gz
        owner = owner_map[brick // n_gy, brick % n_gy]
        return total + jnp.where(owner == my_owner, p_recv[d - 1], 0.0)

    mine = lax.fori_loop(1, peers, add_part, mine)
    for i in range(tall):
        grad_ref[:, i * ny : (i + 1) * ny] = mine[i : i + 1, :]


def on_device(
    e_adjoint, h_adjoint, forward_dft, material, inv_permittivity, conductivity,
    omega, freq_weight, stencil, stencil_weight, owner_map,
):
    nx, nz, ny = material.shape
    freqs = omega.shape[0]
    points = stencil.shape[0]
    n_gx, n_gy, n_gz = (lax.axis_size(a) for a in ("gx", "gy", "gz"))
    peers = n_gx * n_gy * n_gz
    times = (jnp.arange(STEPS) + 1).astype(F32) * time_step
    angles = times[:, None] * omega[None, :]
    phase = jnp.concatenate(
        [freq_weight[None, :] * jnp.cos(angles), -freq_weight[None, :] * jnp.sin(angles)], axis=1
    ).astype(BF16).astype(F32)
    dft = forward_dft.reshape(2 * freqs, 3, nx, nz, ny)
    smem = pl.BlockSpec(memory_space=pltpu.SMEM)
    hbm = pl.BlockSpec(memory_space=pl.ANY)
    vmem = pl.BlockSpec(memory_space=pltpu.VMEM)
    tall = PS // n_gz // ny
    slots = 2 * STEPS
    cell = (nx, nz, ny)
    return pl.pallas_call(
        functools.partial(kernel, n_gx, n_gy, n_gz),
        out_shape=(
            jax.ShapeDtypeStruct(e_adjoint.shape, F32),
            jax.ShapeDtypeStruct(h_adjoint.shape, F32),
            jax.ShapeDtypeStruct((1, PS // n_gz), F32),
        ),
        in_specs=[smem] * 4 + [hbm] * 6,
        out_specs=(vmem, vmem, vmem),
        scratch_shapes=[
            pltpu.VMEM(dft.shape, BF16),
            pltpu.VMEM(cell, jnp.int32),
            pltpu.VMEM(stencil.shape, jnp.int32),
            pltpu.VMEM(stencil_weight.shape, BF16),
            pltpu.VMEM((STEPS, 3) + cell, F32),
            pltpu.VMEM(cell, F32),
            pltpu.VMEM(cell, F32),
            pltpu.VMEM(cell, F32),
            pltpu.VMEM((points, 4, nz, ny), F32),
            pltpu.VMEM((256, 128), F32),
            pltpu.VMEM((PS // LOW, 128), F32),
            pltpu.VMEM((slots, 2, nz, ny), F32),
            pltpu.VMEM((slots, 2 * nx, ny), F32),
            pltpu.VMEM((slots, nz, ny), F32),
            pltpu.VMEM((slots, 2, nz, ny), F32),
            pltpu.VMEM((slots, 2 * nx, ny), F32),
            pltpu.VMEM((slots, nz, ny), F32),
            pltpu.VMEM((STEPS, 2, 8, ny), F32),
            pltpu.VMEM((STEPS, 2, nz, ny), F32),
            pltpu.VMEM((STEPS, 2, 8, ny), F32),
            pltpu.VMEM((STEPS, 2, nz, ny), F32),
            pltpu.VMEM((n_gz, tall, ny), F32),
            pltpu.VMEM((peers - 1, tall, ny), F32),
            pltpu.SemaphoreType.DMA((6,)),
            pltpu.SemaphoreType.DMA((slots, 3)),
            pltpu.SemaphoreType.DMA((slots, 3)),
            pltpu.SemaphoreType.DMA((2, STEPS, 4)),
            pltpu.SemaphoreType.DMA((2,)),
        ],
        compiler_params=pltpu.CompilerParams(
            collective_id=0, has_side_effects=True, vmem_limit_bytes=60 * 1024 * 1024
        ),
    )(phase, inv_permittivity, conductivity, owner_map,
      e_adjoint, h_adjoint, dft, material, stencil, stencil_weight)


def solution(mesh):
    return jax.shard_map(
        on_device,
        mesh=mesh,
        in_specs=(
            P(None, ("parts", "gx"), "gz", "gy"),
            P(None, ("parts", "gx"), "gz", "gy"),
            P(None, None, None, ("parts", "gx"), "gz", "gy"),
            P(("parts", "gx"), "gz", "gy"),
            P(),
            P(),
            P(),
            P(),
            P(None, ("parts", "gx"), "gz", "gy"),
            P(None, ("parts", "gx"), "gz", "gy"),
            P("parts", None),
        ),
        out_specs=(
            P(None, ("parts", "gx"), "gz", "gy"),
            P(None, ("parts", "gx"), "gz", "gy"),
            P(("parts", "gx", "gy"), "gz"),
        ),
        check_vma=False,
    )
```

```python
import functools

import jax
import jax.numpy as jnp
from jax import lax
from jax.experimental import pallas as pl
from jax.experimental.pallas import tpu as pltpu
from jax.sharding import PartitionSpec as P

PS = 1024
STEPS = 4
LOW = 32
time_step = 0.55
MESH = pl.DeviceIdType.MESH
F32 = jnp.float32
BF16 = jnp.bfloat16


def kernel(
    n_gx, n_gy, n_gz,
    phase_re, phase_im, inv_eps, cond, owner_map,
    e_hbm, h_hbm, dft_hbm, mat_hbm, sten_hbm, w_hbm,
    e_ref, h_ref, grad_ref,
    dft, mat, sten, wgt, q_ref, decay_ref, drive_ref, g_ref,
    rows_ref, acc_ref, fold_ref,
    x_send, z_send, y_send, x_recv, z_recv, y_recv,
    row_send, col_send, row_recv, col_recv,
    p_send, p_recv,
    in_sems, send_sems, recv_sems, edge_sems, p_sems,
):
    freqs2, nc, nx, nz, ny = dft.shape
    points = sten.shape[0]
    part = lax.axis_index("parts")
    gx, gy, gz = lax.axis_index("gx"), lax.axis_index("gy"), lax.axis_index("gz")
    peers = n_gx * n_gy * n_gz
    freqs = freqs2 // 2
    me = (gx * n_gy + gy) * n_gz + gz

    def place(rank):
        return (part, rank // (n_gy * n_gz), (rank // n_gz) % n_gy, rank % n_gz)

    loads = [
        pltpu.make_async_copy(src, dst, in_sems.at[i])
        for i, (src, dst) in enumerate(
            [(e_hbm, e_ref), (h_hbm, h_ref), (mat_hbm, mat), (dft_hbm, dft), (sten_hbm, sten), (w_hbm, wgt)]
        )
    ]
    for load in loads:
        load.start()

    barrier = pltpu.get_barrier_semaphore()

    def greet(d, carry):
        pl.semaphore_signal(
            barrier, inc=1, device_id=place(lax.rem(me + d, peers)), device_id_type=MESH
        )
        return carry

    lax.fori_loop(1, peers, greet, 0)

    for has, slots, buf in (
        (gx < n_gx - 1, (0, 2, 4, 6), x_recv), (gx > 0, (1, 3, 5, 7), x_recv),
        (gz < n_gz - 1, (0, 2, 4, 6), z_recv), (gz > 0, (1, 3, 5, 7), z_recv),
        (gy < n_gy - 1, (0, 2, 4, 6), y_recv), (gy > 0, (1, 3, 5, 7), y_recv),
    ):
        @pl.when(jnp.logical_not(has))
        def _():
            for slot in slots:
                buf[slot] = jnp.zeros(buf.shape[1:], F32)

    low = (gx > 0, gy > 0, gz > 0)
    high_side = (gx < n_gx - 1, gy < n_gy - 1, gz < n_gz - 1)
    edges = (
        (row_send, row_recv, 0, 0, 2), (row_send, row_recv, 1, 1, 2),
        (col_send, col_recv, 0, 0, 1), (col_send, col_recv, 1, 1, 0),
    )
    for _, rcv, which, up, down in edges:
        @pl.when(jnp.logical_not(low[up] & high_side[down]))
        def _():
            for step in range(STEPS):
                rcv[step, which] = jnp.zeros(rcv.shape[2:], F32)

    pl.semaphore_wait(barrier, peers - 1)

    lane = lax.broadcasted_iota(jnp.int32, (nz, ny), 1)
    row = lax.broadcasted_iota(jnp.int32, (nz, ny), 0)

    def halo_copies(slot, ahead):
        by = -1 if ahead else 1

        def ends(at, size):
            low, high = at > 0, at < size - 1
            return (low, high) if ahead else (high, low)

        out = []
        for i, (snd, rcv, at, size, to) in enumerate((
            (x_send, x_recv, gx, n_gx, (part, gx + by, gy, gz)),
            (y_send, y_recv, gy, n_gy, (part, gx, gy + by, gz)),
            (z_send, z_recv, gz, n_gz, (part, gx, gy, gz + by)),
        )):
            copy = pltpu.make_async_remote_copy(
                src_ref=snd.at[slot], dst_ref=rcv.at[slot],
                send_sem=send_sems.at[slot, i], recv_sem=recv_sems.at[slot, i],
                device_id=to, device_id_type=MESH,
            )
            sends, receives = ends(at, size)
            out.append((copy, sends, receives))
        return out

    def edge_copies(step):
        out = []
        for i, (snd, rcv, which, up, down) in enumerate(edges):
            to = [gx, gy, gz]
            to[up] = to[up] + 1
            to[down] = to[down] - 1
            copy = pltpu.make_async_remote_copy(
                src_ref=snd.at[step, which], dst_ref=rcv.at[step, which],
                send_sem=edge_sems.at[0, step, i], recv_sem=edge_sems.at[1, step, i],
                device_id=(part, *to), device_id_type=MESH,
            )
            out.append((copy, high_side[up] & low[down], low[up] & high_side[down]))
        return out

    def go(entry):
        @pl.when(entry[1])
        def _():
            entry[0].start()

    def arrive(entry):
        @pl.when(entry[2])
        def _():
            entry[0].wait_recv()

    def start_z(slot, ahead, ref):
        edge_z = 0 if ahead else nz - 1
        for c in range(2):
            for x in range(nx):
                z_send[slot, pl.ds(c * nx + x, 1), :] = ref[c, x, pl.ds(edge_z, 1), :]
        go(halo_copies(slot, ahead)[2])

    def inner_z(comp, x):
        here = e_ref[comp, x]
        return jnp.where(row == nz - 1, 0.0, pltpu.roll(here, nz - 1, 0)) - here

    def start_step(step):
        down, up, lines = halo_copies(2 * step, True), halo_copies(2 * step + 1, False), edge_copies(step)
        end = nx - 1
        for c in range(2):
            x_send[2 * step, c] = e_ref[1 + c, 0]
        go(down[0])
        here = e_ref[0, end]
        turned = pltpu.roll(here, ny - 1, 1)
        x_send[2 * step + 1, 0] = h_ref[1, end] - time_step * (inner_z(0, end) + e_ref[2, end])
        x_send[2 * step + 1, 1] = h_ref[2, end] + time_step * (
            e_ref[1, end] + (jnp.where(lane == ny - 1, 0.0, turned) - here)
        )
        go(up[0])
        col_send[step, 0] = turned
        go(lines[2])
        col_send[step, 1] = pltpu.roll(e_ref[1, 0], (2 * nx - ny) % ny, 1)
        go(lines[3])
        row_send[step, 0] = jnp.broadcast_to(e_ref[0, end, pl.ds(0, 1), :], (8, ny))
        go(lines[0])
        packed = jnp.zeros((nz, ny), F32)
        for c, comp in enumerate((0, 2)):
            for x in range(nx):
                at = c * nx + x
                packed = jnp.where(lane == at, pltpu.roll(e_ref[comp, x], at, 1), packed)
        y_send[2 * step] = packed
        go(down[1])
        packed = jnp.zeros((nz, ny), F32)
        for c in range(2):
            for x in range(nx):
                at = c * nx + x
                if c == 0:
                    value = h_ref[0, x] + time_step * (e_ref[2, x] + inner_z(1, x))
                else:
                    change = e_ref[1, x + 1] - e_ref[1, x] if x < end else -e_ref[1, x]
                    value = h_ref[2, x] - time_step * (change + e_ref[0, x])
                packed = jnp.where(lane == at, pltpu.roll(value, at + 1, 1), packed)
        y_send[2 * step + 1] = packed
        go(up[1])
        line = jnp.zeros((8, ny), F32)
        for x in range(nx):
            line = jnp.where(
                lane[0:8] == x, pltpu.roll(e_ref[1, x, pl.ds(0, 8), :], x + 1, 1), line
            )
        row_send[step, 1] = line
        go(lines[1])
        start_z(2 * step, True, e_ref)

    def finish_step(step):
        for entry in halo_copies(2 * step, True):
            arrive(entry)
        for entry in halo_copies(2 * step + 1, False)[:2] + edge_copies(step):
            arrive(entry)
        slot = 2 * step + 1
        last_row, last_lane = row == nz - 1, lane == ny - 1
        line = jnp.broadcast_to(row_recv[step, 0, pl.ds(0, 1), :], (nz, ny))
        plane = x_recv[slot, 0] + time_step * (e_ref[2, 0] - jnp.where(last_row, line, 0.0))
        x_recv[slot, 0] = jnp.where(gx > 0, plane, 0.0)
        plane = x_recv[slot, 1] - time_step * (
            e_ref[1, 0] - jnp.where(last_lane, col_recv[step, 0], 0.0)
        )
        x_recv[slot, 1] = jnp.where(gx > 0, plane, 0.0)
        own = y_send[2 * step]
        own = jnp.where(lane < nx, -pltpu.roll(own, ny - nx, 1), pltpu.roll(own, nx, 1))
        line = jnp.broadcast_to(row_recv[step, 1, pl.ds(0, 1), :], (nz, ny))
        own = own + jnp.where(last_row & (lane < nx), line, 0.0)
        own = own - jnp.where(lane == 2 * nx - 1, col_recv[step, 1], 0.0)
        y_recv[slot] = jnp.where(gy > 0, y_recv[slot] + time_step * own, 0.0)

    def curl(ref, slot, ahead, x, packed):
        def dx(comp):
            if ahead:
                nxt = ref[comp, x + 1] if x < nx - 1 else x_recv[slot, comp - 1]
                return nxt - ref[comp, x]
            prev = ref[comp, x - 1] if x > 0 else x_recv[slot, comp - 1]
            return ref[comp, x] - prev

        def dz(comp):
            halo = jnp.broadcast_to(z_recv[slot, pl.ds(comp * nx + x, 1), :], (nz, ny))
            here = ref[comp, x]
            if ahead:
                return jnp.where(row == nz - 1, halo, pltpu.roll(here, nz - 1, 0)) - here
            return here - jnp.where(row == 0, halo, pltpu.roll(here, 1, 0))

        def dy(comp):
            at = (comp // 2) * nx + x
            here = ref[comp, x]
            if ahead:
                halo = pltpu.roll(packed, (ny - 1 - at) % ny, 1)
                return jnp.where(lane == ny - 1, halo, pltpu.roll(here, ny - 1, 1)) - here
            halo = pltpu.roll(packed, (ny - at) % ny, 1)
            return here - jnp.where(lane == 0, halo, pltpu.roll(here, 1, 1))

        return dy(2) - dz(1), dz(0) - dx(2), dx(1) - dy(0)

    def weighted(c):
        def body(x, carry):
            sums = [jnp.zeros((nz, ny), F32) for _ in range(STEPS)]
            for f in range(freqs2):
                value = dft[f, c, x].astype(F32)
                for t in range(STEPS):
                    factor = phase_re[t, f] if f < freqs else phase_im[t, f - freqs]
                    sums[t] = sums[t] + factor * value
            for t in range(STEPS):
                q_ref[t, c, x] = sums[t]
            return carry

        lax.fori_loop(0, nx, body, 0)

    loads[0].wait()
    loads[1].wait()
    start_step(0)
    loads[2].wait()
    for x in range(nx):
        which = mat[x]
        inv_cell = jnp.zeros((nz, ny), F32)
        cond_cell = jnp.zeros((nz, ny), F32)
        for m in range(inv_eps.shape[0]):
            inv_cell = jnp.where(which == m, inv_eps[m], inv_cell)
            cond_cell = jnp.where(which == m, cond[m], cond_cell)
        loss = cond_cell * (time_step * 0.5) * inv_cell
        decay_ref[x] = (1.0 - loss) / (1.0 + loss)
        drive_ref[x] = time_step * inv_cell / (1.0 + loss)
        g_ref[x] = jnp.zeros((nz, ny), F32)
    loads[3].wait()
    for c in range(3):
        weighted(c)
    for step in range(STEPS):
        finish_step(step)
        packed = y_recv[2 * step]
        for x in range(nx):
            parts = curl(e_ref, 2 * step, True, x, packed)
            for c in range(3):
                h_ref[c, x] = h_ref[c, x] - time_step * parts[c]
        start_z(2 * step + 1, False, h_ref)
        arrive(halo_copies(2 * step + 1, False)[2])
        packed = y_recv[2 * step + 1]
        for x in range(nx):
            parts = curl(h_ref, 2 * step + 1, False, x, packed)
            decay, drive = decay_ref[x], drive_ref[x]
            for c in range(3):
                e_ref[c, x] = decay * e_ref[c, x] + drive * parts[c]
        if step < STEPS - 1:
            start_step(step + 1)
        for x in range(nx):
            g_ref[x] = g_ref[x] + (
                e_ref[0, x] * q_ref[step, 0, x]
                + e_ref[1, x] * q_ref[step, 1, x]
                + e_ref[2, x] * q_ref[step, 2, x]
            )

    loads[4].wait()
    loads[5].wait()
    high = PS // LOW
    ids = [
        (lax.broadcasted_iota(jnp.int32, (16, ny), 0) + 16 * i).astype(F32).astype(BF16)
        for i in range(2)
    ]
    zero = jnp.zeros((16, ny), BF16)
    one = jnp.ones((16, ny), BF16)
    groups = 4
    acc_ref[...] = jnp.zeros_like(acc_ref)

    def add_points(x, carry):
        total = None
        for k in range(points):
            index = sten[k, x]
            value = wgt[k, x].astype(F32) * g_ref[x]
            top = value.astype(BF16).astype(F32)
            rows_ref[k, 0] = (index >> 5).astype(F32)
            rows_ref[k, 1] = (index & (LOW - 1)).astype(F32)
            rows_ref[k, 2] = top
            rows_ref[k, 3] = value - top
        for k in range(points):
            for pair in range(nz // (2 * groups)):
                upper, rest, lower = [], [], []
                for half in range(2):
                    ups, rests, lows = [], [], []
                    for group in range(groups):
                        z = (group * (nz // (2 * groups)) + pair) * 2 + half
                        wide = [
                            jnp.broadcast_to(rows_ref[k, i, pl.ds(z, 1), :], (16, ny)).astype(BF16)
                            for i in range(4)
                        ]
                        for i in range(2):
                            hit = wide[0] == ids[i]
                            ups.append(jnp.where(hit, wide[2], zero))
                            rests.append(jnp.where(hit, wide[3], zero))
                            lows.append(jnp.where(wide[1] == ids[i], one, zero))
                    upper.append(jnp.concatenate(ups, axis=0))
                    rest.append(jnp.concatenate(rests, axis=0))
                    lower.append(jnp.concatenate(lows, axis=0))
                left = jnp.concatenate(
                    [jnp.concatenate(upper, axis=1), jnp.concatenate(rest, axis=1)], axis=0
                )
                right = jnp.concatenate(lower, axis=1)
                block = lax.dot_general(
                    left, right, (((1,), (1,)), ((), ())), preferred_element_type=F32
                )
                total = block if total is None else total + block
        acc_ref[...] += total
        return carry

    lax.fori_loop(0, nx, add_points, 0)

    pieces = acc_ref[0 : groups * high, :] + acc_ref[groups * high :, :]
    width = groups * LOW
    lane_block = lax.broadcasted_iota(jnp.int32, (high, width), 1) // LOW
    row_block = lax.broadcasted_iota(jnp.int32, (high, width), 0) % groups
    summed = jnp.zeros((high, width), F32)
    for group in range(groups):
        summed = summed + jnp.where(
            lane_block == group, pieces[group * high : (group + 1) * high, :], 0.0
        )
    folded = summed
    for group in range(1, groups):
        folded = folded + pltpu.roll(summed, group * LOW, 1)
    folded = jnp.where(lane_block == row_block, folded, 0.0)
    fold_ref[...] = folded
    flat = fold_ref[pl.ds(0, high // groups, groups), :]
    for group in range(1, groups):
        flat = flat + fold_ref[pl.ds(group, high // groups, groups), :]
    tall = PS // n_gz // ny
    for i in range(n_gz):
        p_send[i] = flat[i * tall : (i + 1) * tall, :]

    def send_part(d, carry):
        to = lax.rem(me + d, peers)
        pltpu.make_async_remote_copy(
            src_ref=p_send.at[to % n_gz], dst_ref=p_recv.at[d - 1],
            send_sem=p_sems.at[0], recv_sem=p_sems.at[1],
            device_id=place(to), device_id_type=MESH,
        ).start()
        return carry

    lax.fori_loop(1, peers, send_part, 0)
    for slot in range(2 * STEPS):
        for copy, sends, _ in halo_copies(slot, slot % 2 == 0):
            @pl.when(sends)
            def _():
                copy.wait_send()
    for step in range(STEPS):
        for copy, sends, _ in edge_copies(step):
            @pl.when(sends)
            def _():
                copy.wait_send()
    pltpu.make_async_copy(p_recv, p_recv, p_sems.at[1]).wait()
    pltpu.make_async_copy(p_recv, p_recv, p_sems.at[0]).wait()

    my_owner = gx * n_gy + gy
    mine = jnp.where(owner_map[gy, gx] == my_owner, p_send[gz], 0.0)

    def add_part(d, total):
        brick = lax.rem(me - d + peers, peers) // n_gz
        owner = owner_map[brick % n_gy, brick // n_gy]
        return total + jnp.where(owner == my_owner, p_recv[d - 1], 0.0)

    mine = lax.fori_loop(1, peers, add_part, mine)
    for i in range(tall):
        grad_ref[:, i * ny : (i + 1) * ny] = mine[i : i + 1, :]


def on_device(
    e_adjoint, h_adjoint, forward_dft, material, inv_permittivity, conductivity,
    omega, freq_weight, stencil, stencil_weight, owner_map,
):
    nx, nz, ny = material.shape
    freqs = omega.shape[0]
    points = stencil.shape[0]
    n_gx, n_gy, n_gz = (lax.axis_size(a) for a in ("gx", "gy", "gz"))
    peers = n_gx * n_gy * n_gz
    times = (jnp.arange(STEPS) + 1).astype(F32) * time_step
    angles = times[:, None] * omega[None, :]
    phase_re = lax.reduce_precision(freq_weight[None, :] * jnp.cos(angles), 8, 7)
    phase_im = lax.reduce_precision(-(freq_weight[None, :] * jnp.sin(angles)), 8, 7)
    dft = forward_dft.reshape(2 * freqs, 3, nx, nz, ny)
    smem = pl.BlockSpec(memory_space=pltpu.SMEM)
    hbm = pl.BlockSpec(memory_space=pl.ANY)
    vmem = pl.BlockSpec(memory_space=pltpu.VMEM)
    tall = PS // n_gz // ny
    slots = 2 * STEPS
    cell = (nx, nz, ny)
    return pl.pallas_call(
        functools.partial(kernel, n_gx, n_gy, n_gz),
        out_shape=(
            jax.ShapeDtypeStruct(e_adjoint.shape, F32),
            jax.ShapeDtypeStruct(h_adjoint.shape, F32),
            jax.ShapeDtypeStruct((1, PS // n_gz), F32),
        ),
        in_specs=[smem] * 5 + [hbm] * 6,
        out_specs=(vmem, vmem, vmem),
        scratch_shapes=[
            pltpu.VMEM(dft.shape, BF16),
            pltpu.VMEM(cell, jnp.int32),
            pltpu.VMEM(stencil.shape, jnp.int32),
            pltpu.VMEM(stencil_weight.shape, BF16),
            pltpu.VMEM((STEPS, 3) + cell, F32),
            pltpu.VMEM(cell, F32),
            pltpu.VMEM(cell, F32),
            pltpu.VMEM(cell, F32),
            pltpu.VMEM((points, 4, nz, ny), F32),
            pltpu.VMEM((256, 128), F32),
            pltpu.VMEM((PS // LOW, 128), F32),
            pltpu.VMEM((slots, 2, nz, ny), F32),
            pltpu.VMEM((slots, 2 * nx, ny), F32),
            pltpu.VMEM((slots, nz, ny), F32),
            pltpu.VMEM((slots, 2, nz, ny), F32),
            pltpu.VMEM((slots, 2 * nx, ny), F32),
            pltpu.VMEM((slots, nz, ny), F32),
            pltpu.VMEM((STEPS, 2, 8, ny), F32),
            pltpu.VMEM((STEPS, 2, nz, ny), F32),
            pltpu.VMEM((STEPS, 2, 8, ny), F32),
            pltpu.VMEM((STEPS, 2, nz, ny), F32),
            pltpu.VMEM((n_gz, tall, ny), F32),
            pltpu.VMEM((peers - 1, tall, ny), F32),
            pltpu.SemaphoreType.DMA((6,)),
            pltpu.SemaphoreType.DMA((slots, 3)),
            pltpu.SemaphoreType.DMA((slots, 3)),
            pltpu.SemaphoreType.DMA((2, STEPS, 4)),
            pltpu.SemaphoreType.DMA((2,)),
        ],
        compiler_params=pltpu.CompilerParams(
            collective_id=0, has_side_effects=True, vmem_limit_bytes=60 * 1024 * 1024
        ),
    )(phase_re, phase_im, inv_permittivity, conductivity, owner_map.T,
      e_adjoint, h_adjoint, dft, material, stencil, stencil_weight)


def solution(mesh):
    return jax.shard_map(
        on_device,
        mesh=mesh,
        in_specs=(
            P(None, ("parts", "gx"), "gz", "gy"),
            P(None, ("parts", "gx"), "gz", "gy"),
            P(None, None, None, ("parts", "gx"), "gz", "gy"),
            P(("parts", "gx"), "gz", "gy"),
            P(),
            P(),
            P(),
            P(),
            P(None, ("parts", "gx"), "gz", "gy"),
            P(None, ("parts", "gx"), "gz", "gy"),
            P("parts", None),
        ),
        out_specs=(
            P(None, ("parts", "gx"), "gz", "gy"),
            P(None, ("parts", "gx"), "gz", "gy"),
            P(("parts", "gx", "gy"), "gz"),
        ),
        check_vma=False,
    )
```
